256 devices in a mesh: grp: 64 (over y, z, core), blk: 4 (over x).
Axes of the slice: x: 4, y: 4, z: 8, core: 2. Of those that a mesh axis runs over, the one named last changes fastest.
Arguments:
- visibility: bfloat16 [64, 4, 64, 32, 2048], P('grp', 'blk'), may hold values from -6 to 6
- block_group: int32 [4, 64], P('blk', 'grp'), may hold values from 0 to 1
- member_valid: int32 [4, 64, 32], P('blk', 'grp'), may hold values 0 or 1
Outputs:
- cross_power: float32 [4, 64, 4, 2, 32, 32, 128], P('blk', 'grp')
The draws below stay inside these ranges and needn't reach their ends.
All inputs are finite; a program needn't handle non-finite values. No bound on the sum of `member_valid` on one device may be relied on, other than what follows from the above.
Results may differ from the reference program's by a relative error of at most 0.0039.
Values may be sent and summed in bfloat16 or wider, within the bound.
A program may use at most 128 MiB of HBM per device.

```python
import math
import jax
import jax.numpy as jnp
from jax import lax

CH = 1024
DBAND = 128
MB = 32
TIMES = 64
NSUB = 4
NCOL = 64


def plant(drawn, stream_key, low, high):
    spot = [jax.random.randint(jax.random.fold_in(stream_key, axis), (), 0, length) for axis, length in enumerate(drawn.shape)]
    longest = drawn.shape.index(max(drawn.shape))
    neighbour = spot[:longest] + [(spot[longest] + 1) % drawn.shape[longest]] + spot[longest + 1:]
    return drawn.at[tuple(spot)].set(low).at[tuple(neighbour)].set(high)


def steps_of(stream_key, shape, cuts, least, largest):
    level, own = 1.0, jax.random.fold_in(stream_key, 6)
    for position, blocks in cuts:
        steps = jnp.exp(jax.random.uniform(jax.random.fold_in(own, position), (blocks,), jnp.float32, least / len(cuts), largest / len(cuts)))
        level = level * jnp.repeat(steps, shape[position] // blocks).reshape([-1 if axis == position else 1 for axis in range(len(shape))])
    return level


def bell_draw(own_key, extent, scale, most, shards=(), held_as=jnp.bfloat16):
    array = jax.random.normal(own_key, extent, jnp.float32) * scale
    if len(shards) > 0:
        array = steps_of(own_key, extent, shards, -0.22, 0.18) * array
    return jnp.clip(array, min=-most, max=most).astype(held_as)


def setup_inputs(seed: int = 0) -> dict:
    keys = jax.random.split(jax.random.key(seed), 4)
    visibility = bell_draw(keys[0], (TIMES, NSUB, NCOL, MB, 2 * CH), 1.0, 6.0, ((0, 64), (1, 4)))
    block_group = plant(jax.random.randint(keys[1], (NSUB, NCOL), 0, 2), jax.random.fold_in(keys[1], 1), 0, 1).astype(jnp.int32)
    member_valid = plant((jax.random.randint(keys[2], (NSUB, NCOL, MB), 0, 4) < 3).astype(jnp.int32), jax.random.fold_in(keys[2], 1), 0, 1)
    return {"visibility": visibility, "block_group": block_group, "member_valid": member_valid}


def delay_table(channels, delay_band):
    channel_index = jnp.arange(channels, dtype=jnp.int32)
    delay_index = jnp.arange(delay_band, dtype=jnp.int32) - delay_band // 2
    angles = 2.0 * math.pi * channel_index.astype(jnp.float32) / channels
    window = 0.35875 - 0.48829 * jnp.cos(angles) + 0.14128 * jnp.cos(2.0 * angles) - 0.01168 * jnp.cos(3.0 * angles)
    turns = jnp.remainder(channel_index[:, None] * delay_index[None, :], channels).astype(jnp.float32)
    phases = 2.0 * math.pi * turns / channels
    scaling = window[:, None] / math.sqrt(channels)
    cosine = scaling * jnp.cos(phases)
    sine_part = scaling * jnp.sin(phases)
    upper_rows = jnp.concatenate([cosine, -sine_part], axis=1)
    lower_rows = jnp.concatenate([sine_part, cosine], axis=1)
    return jnp.concatenate([upper_rows, lower_rows], axis=0).astype(jnp.bfloat16)

def reference(visibility, block_group, member_valid):
    table = delay_table(CH, DBAND).astype(jnp.float32)

    def one_column(column):
        piece = lax.dynamic_slice_in_dim(visibility, column, 1, 2)[:, :, 0]
        spectra = jnp.dot(piece.astype(jnp.float32), table, precision=lax.Precision.HIGHEST, preferred_element_type=jnp.float32)
        spectra = spectra.astype(jnp.bfloat16).astype(jnp.float32)
        real_part = spectra[..., :DBAND]
        imag_part = spectra[..., DBAND:]
        cross_real = jnp.einsum('tsiq,tpjq->spijq', real_part, real_part, precision=lax.Precision.HIGHEST) + jnp.einsum('tsiq,tpjq->spijq', imag_part, imag_part, precision=lax.Precision.HIGHEST)
        cross_imag = jnp.einsum('tsiq,tpjq->spijq', imag_part, real_part, precision=lax.Precision.HIGHEST) - jnp.einsum('tsiq,tpjq->spijq', real_part, imag_part, precision=lax.Precision.HIGHEST)
        labels = lax.dynamic_slice_in_dim(block_group, column, 1, 1)[:, 0]
        valid = lax.dynamic_slice_in_dim(member_valid, column, 1, 1)[:, 0].astype(jnp.float32)
        same_group = (labels[:, None] == labels[None, :]).astype(jnp.float32)
        keeping = same_group[:, :, None, None] * valid[:, None, :, None] * valid[None, :, None, :]
        stacked = jnp.stack([cross_real, cross_imag], axis=2)
        return stacked * keeping[:, :, None, :, :, None] / TIMES
    columns = lax.map(one_column, jnp.arange(NCOL, dtype=jnp.int32))
    return jnp.moveaxis(columns, 0, 1)
```

```python
import functools
import math

import jax
import jax.numpy as jnp
import numpy as np
import ml_dtypes
from jax import lax
from jax.experimental import pallas as pl
from jax.experimental.pallas import tpu as pltpu
from jax.sharding import PartitionSpec as P

MESH = pl.DeviceIdType.MESH
F32 = jnp.float32
BF16 = jnp.bfloat16

CH = 1024
DBAND = 128
MB = 32
NT = 64
NB = 4
NY, NZ = 4, 8
ROWS = 64
LANES = 128
NR = DBAND // 4
CHUNK = 8
NCHUNK = NT // CHUNK
NPAIR = NT // 2
LAG = 8


def delay_table():
    f = np.arange(CH)
    angles = 2.0 * math.pi * f / CH
    window = (
        0.35875
        - 0.48829 * np.cos(angles)
        + 0.14128 * np.cos(2.0 * angles)
        - 0.01168 * np.cos(3.0 * angles)
    ).astype(np.float32)
    d = np.arange(DBAND) - DBAND // 2
    phases = 2.0 * math.pi * ((f[:, None] * d[None, :]) % CH) / CH
    scaling = window[:, None].astype(np.float64) / math.sqrt(CH)
    c, s = scaling * np.cos(phases), scaling * np.sin(phases)
    real = np.concatenate([c, s], axis=0)
    imag = np.concatenate([-s, c], axis=0)
    both = np.stack([real, imag], axis=2).reshape(2 * CH, NR, 4, 2)
    rows = both.transpose(2, 1, 3, 0).reshape(2 * DBAND, 2 * CH)
    return rows.astype(np.float32).astype(ml_dtypes.bfloat16)


def group_masks(shape):
    group = lax.broadcasted_iota(jnp.int32, shape, 1) // MB
    return [group == h for h in range(4)]


def pick(masks, values):
    out = values[3]
    for h in (2, 1, 0):
        out = jnp.where(masks[h], values[h], out)
    return out


def exchange_kernel(
    vis, table, valid, label, gathered, flags,
    vis_v, table_v, valid_v, label_v, turned, send, own_flags,
    vis_sem, table_sem, valid_sem, label_sem, own_sem, flag_own_sem,
    a_s, a_r, x_s, x_r, f_s, f_r, g_s, g_r,
):
    g = lax.axis_index("grp")
    x = lax.axis_index("blk")
    y, z, zh, zl = g // 16, (g // 2) % 8, (g // 8) % 2, (g // 2) % 4
    right, left = (x + 1) % 4, (x + 3) % 4

    def chunk_of(k):
        return ((y + k // 2) % 4) * 2 + (zh + k) % 2

    def vis_copy(k):
        rows = pl.ds(pl.multiple_of(chunk_of(k) * CHUNK * MB, CHUNK * MB), CHUNK * MB)
        return pltpu.make_async_copy(vis.at[rows], vis_v.at[k], vis_sem.at[k])

    table_copy = pltpu.make_async_copy(table, table_v, table_sem)
    valid_copy = pltpu.make_async_copy(valid, valid_v, valid_sem)
    label_copy = pltpu.make_async_copy(label, label_v, label_sem)
    table_copy.start()
    valid_copy.start()
    label_copy.start()
    for k in range(NCHUNK):
        vis_copy(k).start()

    barrier = pltpu.get_barrier_semaphore()

    def greet(i, _):
        pl.semaphore_signal(barrier, inc=1, device_id=((g + i) % NT, x), device_id_type=MESH)
        return 0

    lax.fori_loop(1, NT, greet, 0)
    for o in range(1, NB):
        pl.semaphore_signal(barrier, inc=1, device_id=(g, (x + o) % NB), device_id_type=MESH)

    valid_copy.wait()
    label_copy.wait()
    own_flags[...] = jnp.zeros_like(own_flags)
    own_flags[0:1, :] = jnp.concatenate([valid_v[...]] * 4, axis=1)
    own_flags[1:2, :] = jnp.broadcast_to(label_v[...], (1, LANES))
    table_copy.wait()

    def send_copy(t):
        return pltpu.make_async_remote_copy(
            src_ref=send.at[t], dst_ref=gathered.at[0, g],
            send_sem=a_s.at[t], recv_sem=a_r.at[g],
            device_id=(t, x), device_id_type=MESH,
        )

    def arrival(t):
        return pltpu.make_async_remote_copy(
            src_ref=send.at[t], dst_ref=gathered.at[0, t],
            send_sem=a_s.at[t], recv_sem=a_r.at[t],
            device_id=(t, x), device_id_type=MESH,
        )

    own_copy = pltpu.make_async_copy(send.at[g], gathered.at[0, g], own_sem)
    flag_own = pltpu.make_async_copy(own_flags, flags.at[0], flag_own_sem)
    masks = group_masks((ROWS, LANES))

    def flag_copy(o):
        return pltpu.make_async_remote_copy(
            src_ref=own_flags, dst_ref=flags.at[o],
            send_sem=g_s.at[o], recv_sem=g_r.at[o],
            device_id=(g, (x + NB - o) % NB), device_id_type=MESH,
        )

    def transform(k, _):
        vis_copy(k).wait()
        chunk = chunk_of(k)
        turned[...] = lax.dot_general(
            table_v[...], vis_v[k], (((1,), (1,)), ((), ())), preferred_element_type=F32
        )
        for half in range(2):
            lanes = slice(half * LANES, (half + 1) * LANES)
            parts = [
                turned[pl.ds(pl.multiple_of(((h + NB - x) % 4) * ROWS, ROWS), ROWS), lanes]
                for h in range(4)
            ]
            rolled = []
            for d in range(4):
                v = pick(masks, [parts[(c + d) % 4] for c in range(4)])
                rolled.append(pltpu.roll(v, MB * d, 1) if d else v)
            for c in range(4):
                block = pick(masks, [rolled[(h - c) % 4] for h in range(4)])
                send[chunk * CHUNK + half * 4 + c] = block.astype(BF16)

        @pl.when(k == 0)
        def _():
            pl.semaphore_wait(barrier, NT - 1 + NB - 1)
            own_copy.start()
            flag_own.start()
            for o in range(1, NB):
                flag_copy(o).start()

        for dz in range(4):
            for core in range(2):
                t = chunk * CHUNK + ((zl + dz) % 4) * 2 + core

                @pl.when(t != g)
                def _():
                    send_copy(t).start()

        return 0

    lax.fori_loop(0, NCHUNK, transform, 0)

    def pair_of(k):
        step, dz = k // 4, k % 4
        return ((y + 4 - step // 2) % 4) * 16 + ((zh + step) % 2) * 8 + ((zl + 4 - dz) % 4) * 2

    def x_copy(k, d):
        times = pl.ds(pair_of(k), 2)
        return pltpu.make_async_remote_copy(
            src_ref=gathered.at[0, times], dst_ref=gathered.at[(3, 1)[d], times],
            send_sem=x_s.at[d, k], recv_sem=x_r.at[d, k],
            device_id=(g, (right, left)[d]), device_id_type=MESH,
        )

    def f_copy(k, d):
        times = pl.ds(pair_of(k), 2)
        return pltpu.make_async_remote_copy(
            src_ref=gathered.at[(3, 1)[d], times], dst_ref=gathered.at[2, times],
            send_sem=f_s.at[k], recv_sem=f_r.at[k],
            device_id=(g, (right, left)[d]), device_id_type=MESH,
        )

    def step(k, _):
        @pl.when(k < NPAIR)
        def _():
            for core in range(2):
                t = pair_of(k) + core

                @pl.when(t != g)
                def _():
                    arrival(t).wait_recv()

                @pl.when(t == g)
                def _():
                    own_copy.wait()

            x_copy(k, 0).start()
            x_copy(k, 1).start()

        @pl.when(k >= LAG)
        def _():
            m = k - LAG
            x_copy(m, 0).wait_recv()
            x_copy(m, 1).wait_recv()

            @pl.when(m % 2 == 0)
            def _():
                f_copy(m, 0).start()

            @pl.when(m % 2 == 1)
            def _():
                f_copy(m, 1).start()

        return 0

    lax.fori_loop(0, NPAIR + LAG, step, 0)

    def finish(k, _):
        x_copy(k, 0).wait_send()
        x_copy(k, 1).wait_send()
        f_copy(k, 0).wait_recv()
        f_copy(k, 0).wait_send()
        return 0

    lax.fori_loop(0, NPAIR, finish, 0)

    def sent(i, _):
        send_copy((g + i) % NT).wait_send()
        return 0

    lax.fori_loop(1, NT, sent, 0)
    flag_own.wait()
    for o in range(1, NB):
        flag_copy(o).wait_send()
        flag_copy(o).wait_recv()


def product_kernel(gathered, flags, out, wide, right_v, left_v, prod, out_v, out_sem):
    x = lax.axis_index("blk")

    codes = []
    for o in range(NB):
        same = flags[o, 1:2, :] == flags[0, 1:2, :]
        codes.append(jnp.where(same, flags[o, 0:1, :], 0).astype(F32))
    own_valid = jnp.broadcast_to(flags[0, 0:1, :].astype(F32) / NT, (LANES, LANES)).T
    row_masks = group_masks((1, LANES))
    keep = []
    for ha in range(4):
        code = pick(row_masks, [codes[(hb - ha) % 4] for hb in range(4)])
        keep.append(own_valid[ha * MB : (ha + 1) * MB] * code)

    for o in range(NB):
        for part in range(4):
            wide[pl.ds(part * 1024, 1024), :] = (
                gathered[o, pl.ds(part * 16, 16)].reshape(1024, LANES).astype(F32)
            )

        def relay(r, _):
            real = wide[pl.ds(2 * r, NT, stride=ROWS), :]
            imag = wide[pl.ds(2 * r + 1, NT, stride=ROWS), :]
            right_v[r, 0:NT, o * LANES : (o + 1) * LANES] = real.astype(BF16)
            right_v[r, NT : 2 * NT, o * LANES : (o + 1) * LANES] = imag.astype(BF16)
            if o == 0:
                left_v[r, 0:LANES] = jnp.concatenate([real, imag], axis=0).T.astype(BF16)
                left_v[r, LANES : 2 * LANES] = jnp.concatenate([imag, -real], axis=0).T.astype(BF16)
            return 0

        lax.fori_loop(0, NR, relay, 0, unroll=2)

    masks = group_masks((MB, LANES))

    def multiply(r, _):
        x_all = jnp.dot(left_v[r], right_v[r], preferred_element_type=F32)
        for c in range(2):
            for ha in range(4):
                rows = x_all[c * LANES + ha * MB : c * LANES + (ha + 1) * MB]
                values = []
                for hb in range(4):
                    o = (hb - ha) % 4
                    values.append(rows[:, o * LANES : (o + 1) * LANES])
                place = (r * 4 + (ha + NB - x) % 4) * MB
                prod[c, pl.ds(pl.multiple_of(place, MB), MB), :] = pick(masks, values) * keep[ha]
        return 0

    lax.fori_loop(0, NR, multiply, 0)

    lane = lax.broadcasted_iota(jnp.int32, (MB, LANES), 1) % 4
    delay_masks = [lane == d for d in range(4)]

    def out_copy(n):
        c, i8 = n // 4, n % 4
        return pltpu.make_async_copy(
            out_v.at[:, c, pl.ds(i8 * 8, 8)], out.at[:, c, pl.ds(i8 * 8, 8)], out_sem.at[n]
        )

    for c in range(2):
        for i8 in range(4):

            def turn(ii, _):
                i = i8 * 8 + ii
                flat = prod[c, pl.ds(i, LANES, stride=MB), :].T
                for p in range(NB):
                    values = [flat[((d + p) % 4) * MB : ((d + p) % 4 + 1) * MB] for d in range(4)]
                    out_v[p, c, i] = pick(delay_masks, values)
                return 0

            lax.fori_loop(0, 8, turn, 0, unroll=2)
            out_copy(c * 4 + i8).start()
    for n in range(8):
        out_copy(n).wait()


def local(visibility, block_group, member_valid):
    vis = visibility.reshape(NT * MB, 2 * CH)
    table = jnp.asarray(delay_table())
    dma = pltpu.SemaphoreType.DMA
    hbm_spec = pl.BlockSpec(memory_space=pltpu.HBM)
    vmem_spec = pl.BlockSpec(memory_space=pltpu.VMEM)
    gathered, flags = pl.pallas_call(
        exchange_kernel,
        name="exchange",
        out_shape=(
            jax.ShapeDtypeStruct((NB, NT, ROWS, LANES), BF16),
            jax.ShapeDtypeStruct((NB, 8, LANES), jnp.int32),
        ),
        in_specs=[hbm_spec] * 4,
        out_specs=(vmem_spec, vmem_spec),
        scratch_shapes=[
            pltpu.VMEM((NCHUNK, CHUNK * MB, 2 * CH), BF16),
            pltpu.VMEM((2 * DBAND, 2 * CH), BF16),
            pltpu.VMEM((1, MB), jnp.int32),
            pltpu.VMEM((1, 1), jnp.int32),
            pltpu.VMEM((2 * DBAND, CHUNK * MB), F32),
            pltpu.VMEM((NT, ROWS, LANES), BF16),
            pltpu.VMEM((8, LANES), jnp.int32),
            dma((NCHUNK,)), dma, dma, dma, dma, dma,
            dma((NT,)), dma((NT,)),
            dma((2, NPAIR)), dma((2, NPAIR)),
            dma((NPAIR,)), dma((NPAIR,)),
            dma((NB,)), dma((NB,)),
        ],
        compiler_params=pltpu.CompilerParams(
            collective_id=0, has_side_effects=True, vmem_limit_bytes=119 << 19
        ),
    )(vis, table, member_valid.reshape(1, MB), block_group.reshape(1, 1))
    result = pl.pallas_call(
        product_kernel,
        name="products",
        out_shape=jax.ShapeDtypeStruct((NB, 2, MB, MB, DBAND), F32),
        in_specs=[vmem_spec, vmem_spec],
        out_specs=hbm_spec,
        scratch_shapes=[
            pltpu.VMEM((NT * ROWS, LANES), F32),
            pltpu.VMEM((NR, 2 * NT, NB * LANES), BF16),
            pltpu.VMEM((NR, 2 * LANES, 2 * NT), BF16),
            pltpu.VMEM((2, DBAND * MB, LANES), F32),
            pltpu.VMEM((NB, 2, MB, MB, DBAND), F32),
            dma((8,)),
        ],
        compiler_params=pltpu.CompilerParams(vmem_limit_bytes=40 << 20),
    )(gathered, flags)
    return result[None, None]


def solution(mesh):
    in_specs = (P("grp", "blk", None, None, None), P("blk", "grp"), P("blk", "grp", None))
    out_specs = P("blk", "grp", None, None, None, None, None)
    return jax.shard_map(local, mesh=mesh, in_specs=in_specs, out_specs=out_specs, check_vma=False)
```

```python
import functools
import math

import jax
import jax.numpy as jnp
import numpy as np
import ml_dtypes
from jax import lax
from jax.experimental import pallas as pl
from jax.experimental.pallas import tpu as pltpu
from jax.sharding import PartitionSpec as P

MESH = pl.DeviceIdType.MESH
F32 = jnp.float32
BF16 = jnp.bfloat16

CH = 1024
DBAND = 128
MB = 32
NT = 64
NB = 4
NY, NZ = 4, 8
ROWS = 64
LANES = 128
NR = DBAND // 4
CHUNK = 8
NCHUNK = NT // CHUNK
NCELL = NT // 2
LAG = 8
OTHER = 0
STRIDE = 72


def delay_table():
    f = np.arange(CH)
    angles = 2.0 * math.pi * f / CH
    window = (
        0.35875
        - 0.48829 * np.cos(angles)
        + 0.14128 * np.cos(2.0 * angles)
        - 0.01168 * np.cos(3.0 * angles)
    ).astype(np.float32)
    d = np.arange(DBAND) - DBAND // 2
    phases = 2.0 * math.pi * ((f[:, None] * d[None, :]) % CH) / CH
    scaling = window[:, None].astype(np.float64) / math.sqrt(CH)
    c, s = scaling * np.cos(phases), scaling * np.sin(phases)
    real = np.concatenate([c, s], axis=0)
    imag = np.concatenate([-s, c], axis=0)
    both = np.stack([real, imag], axis=2).reshape(2 * CH, NR, 4, 2)
    rows = both.transpose(2, 1, 3, 0).reshape(2 * DBAND, 2 * CH)
    return rows.astype(np.float32).astype(ml_dtypes.bfloat16)


def entry_class(z):
    return z - (z // 4) * (z - 4)


def group_masks(shape):
    group = lax.broadcasted_iota(jnp.int32, shape, 1) // MB
    return [group == h for h in range(4)]


def pick(masks, values):
    out = values[3]
    for h in (2, 1, 0):
        out = jnp.where(masks[h], values[h], out)
    return out


def exchange_kernel(
    vis, table, valid, label, gathered, flags,
    vis_v, table_v, valid_v, label_v, turned, send, own_flags,
    vis_sem, table_sem, valid_sem, label_sem, own_sem, flag_own_sem,
    present, a_s, a_r, x_s, x_r, f_s, f_r, g_s, g_r,
):
    g = lax.axis_index("grp")
    x = lax.axis_index("blk")
    y, z, zh, zl = g // 16, (g // 2) % 8, (g // 8) % 2, (g // 2) % 4
    right, left = (x + 1) % 4, (x + 3) % 4

    def chunk_of(k):
        return ((y + k) % 4) * 2 + (zh + k // 4) % 2

    def vis_copy(k):
        rows = pl.ds(pl.multiple_of(chunk_of(k) * CHUNK * MB, CHUNK * MB), CHUNK * MB)
        return pltpu.make_async_copy(vis.at[rows], vis_v.at[k], vis_sem.at[k])

    table_copy = pltpu.make_async_copy(table, table_v, table_sem)
    valid_copy = pltpu.make_async_copy(valid, valid_v, valid_sem)
    label_copy = pltpu.make_async_copy(label, label_v, label_sem)
    table_copy.start()
    valid_copy.start()
    label_copy.start()
    for k in range(NCHUNK):
        vis_copy(k).start()

    barrier = pltpu.get_barrier_semaphore()

    mine = entry_class(z)

    def plane(pz, sem):
        for py in range(NY):
            for core in range(2):
                t = py * 16 + pz * 2 + core

                @pl.when(t != g)
                def _():
                    pl.semaphore_signal(sem, inc=1, device_id=(t, x), device_id_type=MESH)

    lax.fori_loop(mine, NZ, lambda pz, _: (plane(pz, barrier), 0)[1], 0)
    for o in range(1, NB):
        pl.semaphore_signal(barrier, inc=1, device_id=(g, (x + o) % NB), device_id_type=MESH)
    last = mine + 1 + (z // 4) * 3
    pl.semaphore_wait(barrier, last * 8 - 1 + NB - 1)
    lax.fori_loop(0, mine, lambda pz, _: (plane(pz, present.at[z]), 0)[1], 0)

    valid_copy.wait()
    label_copy.wait()
    own_flags[...] = jnp.zeros_like(own_flags)
    own_flags[0:1, :] = jnp.concatenate([valid_v[...]] * 4, axis=1)
    own_flags[1:2, :] = jnp.broadcast_to(label_v[...], (1, LANES))
    table_copy.wait()

    def send_copy(t):
        return pltpu.make_async_remote_copy(
            src_ref=send.at[t], dst_ref=gathered.at[0, g],
            send_sem=a_s.at[t], recv_sem=a_r.at[g],
            device_id=(t, x), device_id_type=MESH,
        )

    def arrival(t):
        return pltpu.make_async_remote_copy(
            src_ref=send.at[t], dst_ref=gathered.at[0, t],
            send_sem=a_s.at[t], recv_sem=a_r.at[t],
            device_id=(t, x), device_id_type=MESH,
        )

    own_copy = pltpu.make_async_copy(send.at[g], gathered.at[0, g], own_sem)
    flag_own = pltpu.make_async_copy(own_flags, flags.at[0], flag_own_sem)
    masks = group_masks((ROWS, LANES))

    def flag_copy(o):
        return pltpu.make_async_remote_copy(
            src_ref=own_flags, dst_ref=flags.at[o],
            send_sem=g_s.at[o], recv_sem=g_r.at[o],
            device_id=(g, (x + NB - o) % NB), device_id_type=MESH,
        )

    def send_to(t0, new_plane):
        @pl.when(new_plane & (entry_class((t0 // 2) % 8) > mine))
        def _():
            pl.semaphore_wait(present.at[(t0 // 2) % 8], 8)

        for core in range(2):

            @pl.when(t0 + core != g)
            def _():
                send_copy(t0 + core).start()

    def transform(k, _):
        vis_copy(k).wait()
        chunk = chunk_of(k)
        turned[...] = lax.dot_general(
            table_v[...], vis_v[k], (((1,), (1,)), ((), ())), preferred_element_type=F32
        )
        for half in range(2):
            lanes = slice(half * LANES, (half + 1) * LANES)
            parts = [
                turned[pl.ds(pl.multiple_of(((h + NB - x) % 4) * ROWS, ROWS), ROWS), lanes]
                for h in range(4)
            ]
            rolled = []
            for d in range(4):
                v = pick(masks, [parts[(c + d) % 4] for c in range(4)])
                rolled.append(pltpu.roll(v, MB * d, 1) if d else v)
            for c in range(4):
                block = pick(masks, [rolled[(h - c) % 4] for h in range(4)])
                send[chunk * CHUNK + half * 4 + c] = block.astype(BF16)

        @pl.when(k == 0)
        def _():
            own_copy.start()
            flag_own.start()
            for o in range(1, NB):
                flag_copy(o).start()

        @pl.when(k < 4)
        def _():
            for dz in range(4):
                send_to(chunk * CHUNK + ((zl + dz) % 4) * 2, k == 0)

        return 0

    lax.fori_loop(0, NCHUNK, transform, 0)

    def pair_of(k):
        dy, dz = (k // 4) % 4, k % 4
        return ((y + 4 - dy) % 4) * 16 + ((zh + k // 16) % 2) * 8 + ((zl + 4 - dz) % 4) * 2

    def x_copy(k, d):
        times = pl.ds(pair_of(k), 2)
        return pltpu.make_async_remote_copy(
            src_ref=gathered.at[0, times], dst_ref=gathered.at[(3, 1)[d], times],
            send_sem=x_s.at[d, k], recv_sem=x_r.at[d, k],
            device_id=(g, (right, left)[d]), device_id_type=MESH,
        )

    def f_copy(k, d):
        times = pl.ds(pair_of(k), 2)
        return pltpu.make_async_remote_copy(
            src_ref=gathered.at[(3, 1)[d], times], dst_ref=gathered.at[2, times],
            send_sem=f_s.at[k], recv_sem=f_r.at[k],
            device_id=(g, (right, left)[d]), device_id_type=MESH,
        )

    def step(k, _):
        @pl.when((k >= OTHER) & (k < OTHER + 16))
        def _():
            n = k - OTHER
            send_to(chunk_of(4 + n // 4) * CHUNK + ((zl + n % 4) % 4) * 2, n < 4)

        @pl.when(k < NCELL)
        def _():
            for core in range(2):
                t = pair_of(k) + core

                @pl.when(t != g)
                def _():
                    arrival(t).wait_recv()

                @pl.when(t == g)
                def _():
                    own_copy.wait()

            x_copy(k, 0).start()
            x_copy(k, 1).start()

        @pl.when(k >= LAG)
        def _():
            m = k - LAG
            x_copy(m, 0).wait_recv()
            x_copy(m, 1).wait_recv()

            @pl.when(m % 2 == 0)
            def _():
                f_copy(m, 0).start()

            @pl.when(m % 2 == 1)
            def _():
                f_copy(m, 1).start()

        return 0

    lax.fori_loop(0, NCELL + LAG, step, 0)

    def finish(k, _):
        x_copy(k, 0).wait_send()
        x_copy(k, 1).wait_send()
        f_copy(k, 0).wait_recv()
        f_copy(k, 0).wait_send()
        return 0

    lax.fori_loop(0, NCELL, finish, 0)

    def sent(i, _):
        send_copy((g + i) % NT).wait_send()
        return 0

    lax.fori_loop(1, NT, sent, 0)
    flag_own.wait()
    for o in range(1, NB):
        flag_copy(o).wait_send()
        flag_copy(o).wait_recv()


def product_kernel(gathered, flags, out, wide, right_v, left_v, prod, out_v, out_sem):
    x = lax.axis_index("blk")

    codes = []
    for o in range(NB):
        same = flags[o, 1:2, :] == flags[0, 1:2, :]
        codes.append(jnp.where(same, flags[o, 0:1, :], 0).astype(F32))
    own_valid = jnp.broadcast_to(flags[0, 0:1, :].astype(F32) / NT, (LANES, LANES)).T
    row_masks = group_masks((1, LANES))
    keep = []
    for ha in range(4):
        code = pick(row_masks, [codes[(hb - ha) % 4] for hb in range(4)])
        keep.append(own_valid[ha * MB : (ha + 1) * MB] * code)

    for o in range(NB):
        def widen(t, _):
            rows = pl.ds(pl.multiple_of(t * STRIDE, 8), ROWS)
            wide[rows, :] = gathered[o, t].astype(F32)
            return 0

        lax.fori_loop(0, NT, widen, 0, unroll=8)

        def relay(r, _):
            real = wide[pl.ds(2 * r, NT, stride=STRIDE), :]
            imag = wide[pl.ds(2 * r + 1, NT, stride=STRIDE), :]
            right_v[r, 0:NT, o * LANES : (o + 1) * LANES] = real.astype(BF16)
            right_v[r, NT : 2 * NT, o * LANES : (o + 1) * LANES] = imag.astype(BF16)
            if o == 0:
                left_v[r, 0:LANES] = jnp.concatenate([real, imag], axis=0).T.astype(BF16)
                left_v[r, LANES : 2 * LANES] = jnp.concatenate([imag, -real], axis=0).T.astype(BF16)
            return 0

        lax.fori_loop(0, NR, relay, 0, unroll=8)

    masks = group_masks((MB, LANES))

    def multiply(r, _):
        x_all = jnp.dot(left_v[r], right_v[r], preferred_element_type=F32)
        for c in range(2):
            for ha in range(4):
                rows = x_all[c * LANES + ha * MB : c * LANES + (ha + 1) * MB]
                values = []
                for hb in range(4):
                    o = (hb - ha) % 4
                    values.append(rows[:, o * LANES : (o + 1) * LANES])
                place = (r * 4 + (ha + NB - x) % 4) * MB
                prod[c, pl.ds(pl.multiple_of(place, MB), MB), :] = pick(masks, values) * keep[ha]
        return 0

    lax.fori_loop(0, NR, multiply, 0, unroll=8)

    lane = lax.broadcasted_iota(jnp.int32, (MB, LANES), 1) % 4
    delay_masks = [lane == d for d in range(4)]

    def out_copy(n):
        c, i8 = n // 4, n % 4
        return pltpu.make_async_copy(
            out_v.at[:, c, pl.ds(i8 * 8, 8)], out.at[:, c, pl.ds(i8 * 8, 8)], out_sem.at[n]
        )

    for c in range(2):
        for i8 in range(4):

            def turn(ii, _):
                i = i8 * 8 + ii
                flat = prod[c, pl.ds(i, LANES, stride=MB), :].T
                for p in range(NB):
                    values = [flat[((d + p) % 4) * MB : ((d + p) % 4 + 1) * MB] for d in range(4)]
                    out_v[p, c, i] = pick(delay_masks, values)
                return 0

            lax.fori_loop(0, 8, turn, 0, unroll=8)
            out_copy(c * 4 + i8).start()
    for n in range(8):
        out_copy(n).wait()


def local(visibility, block_group, member_valid):
    vis = visibility.reshape(NT * MB, 2 * CH)
    table = jnp.asarray(delay_table())
    dma = pltpu.SemaphoreType.DMA
    hbm_spec = pl.BlockSpec(memory_space=pltpu.HBM)
    vmem_spec = pl.BlockSpec(memory_space=pltpu.VMEM)
    gathered, flags = pl.pallas_call(
        exchange_kernel,
        name="exchange",
        out_shape=(
            jax.ShapeDtypeStruct((NB, NT, ROWS, LANES), BF16),
            jax.ShapeDtypeStruct((NB, 8, LANES), jnp.int32),
        ),
        in_specs=[hbm_spec] * 4,
        out_specs=(vmem_spec, vmem_spec),
        scratch_shapes=[
            pltpu.VMEM((NCHUNK, CHUNK * MB, 2 * CH), BF16),
            pltpu.VMEM((2 * DBAND, 2 * CH), BF16),
            pltpu.VMEM((1, MB), jnp.int32),
            pltpu.VMEM((1, 1), jnp.int32),
            pltpu.VMEM((2 * DBAND, CHUNK * MB), F32),
            pltpu.VMEM((NT, ROWS, LANES), BF16),
            pltpu.VMEM((8, LANES), jnp.int32),
            dma((NCHUNK,)), dma, dma, dma, dma, dma,
            pltpu.SemaphoreType.REGULAR((NZ,)),
            dma((NT,)), dma((NT,)),
            dma((2, NCELL)), dma((2, NCELL)),
            dma((NCELL,)), dma((NCELL,)),
            dma((NB,)), dma((NB,)),
        ],
        compiler_params=pltpu.CompilerParams(
            collective_id=0, has_side_effects=True, vmem_limit_bytes=119 << 19
        ),
    )(vis, table, member_valid.reshape(1, MB), block_group.reshape(1, 1))
    result = pl.pallas_call(
        product_kernel,
        name="products",
        out_shape=jax.ShapeDtypeStruct((NB, 2, MB, MB, DBAND), F32),
        in_specs=[vmem_spec, vmem_spec],
        out_specs=hbm_spec,
        scratch_shapes=[
            pltpu.VMEM((NT * STRIDE, LANES), F32),
            pltpu.VMEM((NR, 2 * NT, NB * LANES), BF16),
            pltpu.VMEM((NR, 2 * LANES, 2 * NT), BF16),
            pltpu.VMEM((2, DBAND * MB, LANES), F32),
            pltpu.VMEM((NB, 2, MB, MB, DBAND), F32),
            dma((8,)),
        ],
        compiler_params=pltpu.CompilerParams(vmem_limit_bytes=40 << 20),
    )(gathered, flags)
    return result[None, None]


def solution(mesh):
    in_specs = (P("grp", "blk", None, None, None), P("blk", "grp"), P("blk", "grp", None))
    out_specs = P("blk", "grp", None, None, None, None, None)
    return jax.shard_map(local, mesh=mesh, in_specs=in_specs, out_specs=out_specs, check_vma=False)
```

```python
import functools
import math

import jax
import jax.numpy as jnp
import numpy as np
import ml_dtypes
from jax import lax
from jax.experimental import pallas as pl
from jax.experimental.pallas import tpu as pltpu
from jax.sharding import PartitionSpec as P

MESH = pl.DeviceIdType.MESH
F32 = jnp.float32
BF16 = jnp.bfloat16

CH = 1024
DBAND = 128
MB = 32
NT = 64
NB = 4
NY, NZ = 4, 8
ROWS = 64
LANES = 128
NR = DBAND // 4
CHUNK = 8
NCHUNK = NT // CHUNK
NCELL = NT // 2
LAG = 8
DELAY = 3
EXCHANGE_VMEM = 48 << 20
TURN_VMEM = 16 << 20
STRIDE = 72


def delay_table():
    f = np.arange(CH)
    angles = 2.0 * math.pi * f / CH
    window = (
        0.35875
        - 0.48829 * np.cos(angles)
        + 0.14128 * np.cos(2.0 * angles)
        - 0.01168 * np.cos(3.0 * angles)
    ).astype(np.float32)
    d = np.arange(DBAND) - DBAND // 2
    phases = 2.0 * math.pi * ((f[:, None] * d[None, :]) % CH) / CH
    scaling = window[:, None].astype(np.float64) / math.sqrt(CH)
    c, s = scaling * np.cos(phases), scaling * np.sin(phases)
    real = np.concatenate([c, s], axis=0)
    imag = np.concatenate([-s, c], axis=0)
    both = np.stack([real, imag], axis=2).reshape(2 * CH, NR, 4, 2)
    rows = both.transpose(2, 1, 3, 0).reshape(2 * DBAND, 2 * CH)
    return rows.astype(np.float32).astype(ml_dtypes.bfloat16)


def entry_class(z):
    return z - (z // 4) * (z - 4)


def group_masks(shape):
    group = lax.broadcasted_iota(jnp.int32, shape, 1) // MB
    return [group == h for h in range(4)]


def pick(masks, values):
    out = values[3]
    for h in (2, 1, 0):
        out = jnp.where(masks[h], values[h], out)
    return out


def exchange_kernel(
    vis, table, valid, label, prod,
    vis_v, table_v, valid_v, label_v, turned, send, own_flags, flags, gathered, wide, right_v, left_v,
    vis_sem, table_sem, valid_sem, label_sem, own_sem, flag_own_sem,
    present, a_s, a_r, x_s, x_r, f_s, f_r, g_s, g_r,
):
    g = lax.axis_index("grp")
    x = lax.axis_index("blk")
    y, z, zh, zl = g // 16, (g // 2) % 8, (g // 8) % 2, (g // 2) % 4
    right, left = (x + 1) % 4, (x + 3) % 4

    def chunk_of(k):
        return ((y + k) % 4) * 2 + (zh + k // 4) % 2

    def vis_copy(k):
        rows = pl.ds(pl.multiple_of(chunk_of(k) * CHUNK * MB, CHUNK * MB), CHUNK * MB)
        return pltpu.make_async_copy(vis.at[rows], vis_v.at[k], vis_sem.at[k])

    table_copy = pltpu.make_async_copy(table, table_v, table_sem)
    valid_copy = pltpu.make_async_copy(valid, valid_v, valid_sem)
    label_copy = pltpu.make_async_copy(label, label_v, label_sem)
    table_copy.start()
    valid_copy.start()
    label_copy.start()
    for k in range(NCHUNK):
        vis_copy(k).start()

    barrier = pltpu.get_barrier_semaphore()

    mine = entry_class(z)

    def plane(pz, sem):
        for py in range(NY):
            for core in range(2):
                t = py * 16 + pz * 2 + core

                @pl.when(t != g)
                def _():
                    pl.semaphore_signal(sem, inc=1, device_id=(t, x), device_id_type=MESH)

    lax.fori_loop(mine, NZ, lambda pz, _: (plane(pz, barrier), 0)[1], 0)
    for o in range(1, NB):
        pl.semaphore_signal(barrier, inc=1, device_id=(g, (x + o) % NB), device_id_type=MESH)
    last = mine + 1 + (z // 4) * 3
    pl.semaphore_wait(barrier, last * 8 - 1 + NB - 1)
    lax.fori_loop(0, mine, lambda pz, _: (plane(pz, present.at[z]), 0)[1], 0)

    valid_copy.wait()
    label_copy.wait()
    own_flags[...] = jnp.zeros_like(own_flags)
    own_flags[0:1, :] = jnp.concatenate([valid_v[...]] * 4, axis=1)
    own_flags[1:2, :] = jnp.broadcast_to(label_v[...], (1, LANES))
    table_copy.wait()

    def send_copy(t):
        return pltpu.make_async_remote_copy(
            src_ref=send.at[t], dst_ref=gathered.at[0, g],
            send_sem=a_s.at[t], recv_sem=a_r.at[g],
            device_id=(t, x), device_id_type=MESH,
        )

    def arrival(t):
        return pltpu.make_async_remote_copy(
            src_ref=send.at[t], dst_ref=gathered.at[0, t],
            send_sem=a_s.at[t], recv_sem=a_r.at[t],
            device_id=(t, x), device_id_type=MESH,
        )

    own_copy = pltpu.make_async_copy(send.at[g], gathered.at[0, g], own_sem)
    flag_own = pltpu.make_async_copy(own_flags, flags.at[0], flag_own_sem)
    masks = group_masks((ROWS, LANES))

    def flag_copy(o):
        return pltpu.make_async_remote_copy(
            src_ref=own_flags, dst_ref=flags.at[o],
            send_sem=g_s.at[o], recv_sem=g_r.at[o],
            device_id=(g, (x + NB - o) % NB), device_id_type=MESH,
        )

    def send_to(t0, new_plane):
        @pl.when(new_plane & (entry_class((t0 // 2) % 8) > mine))
        def _():
            pl.semaphore_wait(present.at[(t0 // 2) % 8], 8)

        for core in range(2):

            @pl.when(t0 + core != g)
            def _():
                send_copy(t0 + core).start()

    def transform(k, _):
        vis_copy(k).wait()
        chunk = chunk_of(k)
        turned[...] = lax.dot_general(
            table_v[...], vis_v[k], (((1,), (1,)), ((), ())), preferred_element_type=F32
        )
        for half in range(2):
            lanes = slice(half * LANES, (half + 1) * LANES)
            parts = [
                turned[pl.ds(pl.multiple_of(((h + NB - x) % 4) * ROWS, ROWS), ROWS), lanes]
                for h in range(4)
            ]
            rolled = []
            for d in range(4):
                v = pick(masks, [parts[(c + d) % 4] for c in range(4)])
                rolled.append(pltpu.roll(v, MB * d, 1) if d else v)
            for c in range(4):
                block = pick(masks, [rolled[(h - c) % 4] for h in range(4)])
                send[chunk * CHUNK + half * 4 + c] = block.astype(BF16)

        @pl.when(k == 0)
        def _():
            own_copy.start()
            flag_own.start()
            for o in range(1, NB):
                flag_copy(o).start()

        for dz in range(4):
            send_to(chunk * CHUNK + ((zl + dz) % 4) * 2, k % 4 == 0)

        @pl.when(k >= DELAY)
        def _():
            lax.fori_loop(4 * (k - DELAY), 4 * (k - DELAY + 1), step, 0)

        return 0

    def pair_of(k):
        dy, dz = (k // 4) % 4, k % 4
        return ((y + 4 - dy) % 4) * 16 + ((zh + k // 16) % 2) * 8 + ((zl + 4 - dz) % 4) * 2

    def x_copy(k, d):
        times = pl.ds(pair_of(k), 2)
        return pltpu.make_async_remote_copy(
            src_ref=gathered.at[0, times], dst_ref=gathered.at[(3, 1)[d], times],
            send_sem=x_s.at[d, k], recv_sem=x_r.at[d, k],
            device_id=(g, (right, left)[d]), device_id_type=MESH,
        )

    def f_copy(k, d):
        times = pl.ds(pair_of(k), 2)
        return pltpu.make_async_remote_copy(
            src_ref=gathered.at[(3, 1)[d], times], dst_ref=gathered.at[2, times],
            send_sem=f_s.at[k], recv_sem=f_r.at[k],
            device_id=(g, (right, left)[d]), device_id_type=MESH,
        )

    def step(k, _):
        @pl.when(k < NCELL)
        def _():
            for core in range(2):
                t = pair_of(k) + core

                @pl.when(t != g)
                def _():
                    arrival(t).wait_recv()

                @pl.when(t == g)
                def _():
                    own_copy.wait()

            x_copy(k, 0).start()
            x_copy(k, 1).start()

        @pl.when(k >= LAG)
        def _():
            m = k - LAG
            x_copy(m, 0).wait_recv()
            x_copy(m, 1).wait_recv()

            @pl.when(m % 2 == 0)
            def _():
                f_copy(m, 0).start()

            @pl.when(m % 2 == 1)
            def _():
                f_copy(m, 1).start()

        return 0

    lax.fori_loop(0, NCHUNK, transform, 0)
    lax.fori_loop(4 * (NCHUNK - DELAY), NCELL, step, 0)

    flag_own.wait()
    for o in range(1, NB):
        flag_copy(o).wait_recv()
    keep = keep_masks(flags)
    place_masks = group_masks((MB, LANES))

    def products(o):
        def widen(t, _):
            rows = pl.ds(pl.multiple_of(t * STRIDE, 8), ROWS)
            wide[rows, :] = gathered[o, t].astype(F32)
            return 0

        lax.fori_loop(0, NT, widen, 0, unroll=8)

        def relay(r, _):
            real = wide[pl.ds(2 * r, NT, stride=STRIDE), :]
            imag = wide[pl.ds(2 * r + 1, NT, stride=STRIDE), :]
            right_v[r, 0:NT] = real.astype(BF16)
            right_v[r, NT : 2 * NT] = imag.astype(BF16)
            if o == 0:
                left_v[r, 0:LANES] = jnp.concatenate([real, imag], axis=0).T.astype(BF16)
                left_v[r, LANES : 2 * LANES] = jnp.concatenate([imag, -real], axis=0).T.astype(BF16)
            return 0

        lax.fori_loop(0, NR, relay, 0, unroll=8)

        def multiply(r, _):
            x_all = jnp.dot(left_v[r], right_v[r], preferred_element_type=F32)
            for c in range(2):
                for ha in range(4):
                    rows = x_all[c * LANES + ha * MB : c * LANES + (ha + 1) * MB] * keep[ha]
                    place = (r * 4 + (ha + NB - x) % 4) * MB
                    pltpu.store(
                        prod.at[c, pl.ds(pl.multiple_of(place, MB), MB), :],
                        rows, mask=place_masks[(ha + o) % 4],
                    )
            return 0

        lax.fori_loop(0, NR, multiply, 0, unroll=8)

    products(0)
    lax.fori_loop(NCELL, NCELL + LAG, step, 0)
    products(1)
    products(3)

    def finish(k, _):
        x_copy(k, 0).wait_send()
        x_copy(k, 1).wait_send()
        f_copy(k, 0).wait_recv()
        f_copy(k, 0).wait_send()
        return 0

    lax.fori_loop(0, NCELL, finish, 0)
    products(2)

    def sent(i, _):
        send_copy((g + i) % NT).wait_send()
        return 0

    lax.fori_loop(1, NT, sent, 0)
    for o in range(1, NB):
        flag_copy(o).wait_send()


def keep_masks(flags):
    codes = []
    for o in range(NB):
        same = flags[o, 1:2, :] == flags[0, 1:2, :]
        codes.append(jnp.where(same, flags[o, 0:1, :], 0).astype(F32))
    own_valid = jnp.broadcast_to(flags[0, 0:1, :].astype(F32) / NT, (LANES, LANES)).T
    row_masks = group_masks((1, LANES))
    keep = []
    for ha in range(4):
        code = pick(row_masks, [codes[(hb - ha) % 4] for hb in range(4)])
        keep.append(own_valid[ha * MB : (ha + 1) * MB] * code)
    return keep


def turn_kernel(prod, out, out_v, out_sem):
    lane = lax.broadcasted_iota(jnp.int32, (MB, LANES), 1) % 4
    delay_masks = [lane == d for d in range(4)]

    def out_copy(n):
        c, i8 = n // 4, n % 4
        return pltpu.make_async_copy(
            out_v.at[:, c, pl.ds(i8 * 8, 8)], out.at[:, c, pl.ds(i8 * 8, 8)], out_sem.at[n]
        )

    for c in range(2):
        for i8 in range(4):

            def turn(ii, _):
                i = i8 * 8 + ii
                flat = prod[c, pl.ds(i, LANES, stride=MB), :].T
                for p in range(NB):
                    values = [flat[((d + p) % 4) * MB : ((d + p) % 4 + 1) * MB] for d in range(4)]
                    out_v[p, c, i] = pick(delay_masks, values)
                return 0

            lax.fori_loop(0, 8, turn, 0, unroll=8)
            out_copy(c * 4 + i8).start()
    for n in range(8):
        out_copy(n).wait()


def local(visibility, block_group, member_valid):
    vis = visibility.reshape(NT * MB, 2 * CH)
    table = jnp.asarray(delay_table())
    dma = pltpu.SemaphoreType.DMA
    hbm_spec = pl.BlockSpec(memory_space=pltpu.HBM)
    vmem_spec = pl.BlockSpec(memory_space=pltpu.VMEM)
    prod = pl.pallas_call(
        exchange_kernel,
        name="exchange",
        out_shape=jax.ShapeDtypeStruct((2, DBAND * MB, LANES), F32),
        in_specs=[hbm_spec] * 4,
        out_specs=vmem_spec,
        scratch_shapes=[
            pltpu.VMEM((NCHUNK, CHUNK * MB, 2 * CH), BF16),
            pltpu.VMEM((2 * DBAND, 2 * CH), BF16),
            pltpu.VMEM((1, MB), jnp.int32),
            pltpu.VMEM((1, 1), jnp.int32),
            pltpu.VMEM((2 * DBAND, CHUNK * MB), F32),
            pltpu.VMEM((NT, ROWS, LANES), BF16),
            pltpu.VMEM((8, LANES), jnp.int32),
            pltpu.VMEM((NB, 8, LANES), jnp.int32),
            pltpu.VMEM((NB, NT, ROWS, LANES), BF16),
            pltpu.VMEM((NT * STRIDE, LANES), F32),
            pltpu.VMEM((NR, 2 * NT, LANES), BF16),
            pltpu.VMEM((NR, 2 * LANES, 2 * NT), BF16),
            dma((NCHUNK,)), dma, dma, dma, dma, dma,
            pltpu.SemaphoreType.REGULAR((NZ,)),
            dma((NT,)), dma((NT,)),
            dma((2, NCELL)), dma((2, NCELL)),
            dma((NCELL,)), dma((NCELL,)),
            dma((NB,)), dma((NB,)),
        ],
        compiler_params=pltpu.CompilerParams(
            collective_id=0, has_side_effects=True, vmem_limit_bytes=EXCHANGE_VMEM
        ),
    )(
        *(
            pltpu.with_memory_space_constraint(a, pltpu.HBM)
            for a in (vis, table, member_valid.reshape(1, MB))
        ),
        block_group.reshape(1, 1),
    )
    result = pl.pallas_call(
        turn_kernel,
        name="turn",
        out_shape=jax.ShapeDtypeStruct((NB, 2, MB, MB, DBAND), F32),
        in_specs=[vmem_spec],
        out_specs=hbm_spec,
        scratch_shapes=[pltpu.VMEM((NB, 2, MB, MB, DBAND), F32), dma((8,))],
        compiler_params=pltpu.CompilerParams(vmem_limit_bytes=TURN_VMEM),
    )(prod)
    return result[None, None]


def solution(mesh):
    in_specs = (P("grp", "blk", None, None, None), P("blk", "grp"), P("blk", "grp", None))
    out_specs = P("blk", "grp", None, None, None, None, None)
    return jax.shard_map(local, mesh=mesh, in_specs=in_specs, out_specs=out_specs, check_vma=False)
```

```python
import functools
import math

import jax
import jax.numpy as jnp
import numpy as np
import ml_dtypes
from jax import lax
from jax.experimental import pallas as pl
from jax.experimental.pallas import tpu as pltpu
from jax.sharding import PartitionSpec as P

MESH = pl.DeviceIdType.MESH
F32 = jnp.float32
BF16 = jnp.bfloat16

CH = 1024
DBAND = 128
MB = 32
NT = 64
NB = 4
NY, NZ = 4, 8
ROWS = 64
LANES = 128
NR = DBAND // 4
CHUNK = 8
NCHUNK = NT // CHUNK
NCELL = NT // 2
LAG = 8
DELAY = 3
EXCHANGE_VMEM = 48 << 20
TURN_VMEM = 16 << 20
STRIDE = 72


def delay_table():
    f = np.arange(CH)
    angles = 2.0 * math.pi * f / CH
    window = (
        0.35875
        - 0.48829 * np.cos(angles)
        + 0.14128 * np.cos(2.0 * angles)
        - 0.01168 * np.cos(3.0 * angles)
    ).astype(np.float32)
    d = np.arange(DBAND) - DBAND // 2
    phases = 2.0 * math.pi * ((f[:, None] * d[None, :]) % CH) / CH
    scaling = window[:, None].astype(np.float64) / math.sqrt(CH)
    c, s = scaling * np.cos(phases), scaling * np.sin(phases)
    real = np.concatenate([c, s], axis=0)
    imag = np.concatenate([-s, c], axis=0)
    both = np.stack([real, imag], axis=2).reshape(2 * CH, NR, 4, 2)
    rows = both.transpose(2, 1, 3, 0).reshape(2 * DBAND, 2 * CH)
    return rows.astype(np.float32).astype(ml_dtypes.bfloat16)


def entry_class(z):
    return z - (z // 4) * (z - 4)


def group_masks(shape):
    group = lax.broadcasted_iota(jnp.int32, shape, 1) // MB
    return [group == h for h in range(4)]


def pick(masks, values):
    out = values[3]
    for h in (2, 1, 0):
        out = jnp.where(masks[h], values[h], out)
    return out


def exchange_kernel(
    vis, table, valid, label, prod,
    vis_v, table_v, valid_v, label_v, turned, send, own_flags, flags, gathered, wide, right_v, left_v,
    vis_sem, table_sem, valid_sem, label_sem, own_sem, flag_own_sem,
    present, a_s, a_r, x_s, x_r, f_s, f_r, g_s, g_r,
):
    g = lax.axis_index("grp")
    x = lax.axis_index("blk")
    y, z, zh, zl = g // 16, (g // 2) % 8, (g // 8) % 2, (g // 2) % 4
    right, left = (x + 1) % 4, (x + 3) % 4

    def chunk_of(k):
        return ((y + k) % 4) * 2 + (zh + k // 4) % 2

    def vis_copy(k):
        rows = pl.ds(pl.multiple_of(chunk_of(k) * CHUNK * MB, CHUNK * MB), CHUNK * MB)
        return pltpu.make_async_copy(vis.at[rows], vis_v.at[k], vis_sem.at[k])

    table_copy = pltpu.make_async_copy(table, table_v, table_sem)
    valid_copy = pltpu.make_async_copy(valid, valid_v, valid_sem)
    label_copy = pltpu.make_async_copy(label, label_v, label_sem)
    table_copy.start()
    valid_copy.start()
    label_copy.start()
    for k in range(NCHUNK):
        vis_copy(k).start()

    barrier = pltpu.get_barrier_semaphore()

    mine = entry_class(z)

    def plane(pz, sem):
        for py in range(NY):
            for core in range(2):
                t = py * 16 + pz * 2 + core

                @pl.when(t != g)
                def _():
                    pl.semaphore_signal(sem, inc=1, device_id=(t, x), device_id_type=MESH)

    lax.fori_loop(mine, NZ, lambda pz, _: (plane(pz, barrier), 0)[1], 0)
    for o in range(1, NB):
        pl.semaphore_signal(barrier, inc=1, device_id=(g, (x + o) % NB), device_id_type=MESH)
    last = mine + 1 + (z // 4) * 3
    pl.semaphore_wait(barrier, last * 8 - 1 + NB - 1)
    lax.fori_loop(0, mine, lambda pz, _: (plane(pz, present.at[z]), 0)[1], 0)

    valid_copy.wait()
    label_copy.wait()
    own_flags[...] = jnp.zeros_like(own_flags)
    own_flags[0:1, :] = jnp.concatenate([valid_v[...]] * 4, axis=1)
    own_flags[1:2, :] = jnp.broadcast_to(label_v[...], (1, LANES))
    table_copy.wait()

    def send_copy(t):
        return pltpu.make_async_remote_copy(
            src_ref=send.at[t], dst_ref=gathered.at[0, g],
            send_sem=a_s, recv_sem=a_r.at[g],
            device_id=(t, x), device_id_type=MESH,
        )

    def arrival(t):
        return pltpu.make_async_remote_copy(
            src_ref=send.at[t], dst_ref=gathered.at[0, t],
            send_sem=a_s, recv_sem=a_r.at[t],
            device_id=(t, x), device_id_type=MESH,
        )

    own_copy = pltpu.make_async_copy(send.at[g], gathered.at[0, g], own_sem)
    flag_own = pltpu.make_async_copy(own_flags, flags.at[0], flag_own_sem)
    masks = group_masks((ROWS, LANES))

    def flag_copy(o):
        return pltpu.make_async_remote_copy(
            src_ref=own_flags, dst_ref=flags.at[o],
            send_sem=g_s.at[o], recv_sem=g_r.at[o],
            device_id=(g, (x + NB - o) % NB), device_id_type=MESH,
        )

    def send_to(t0, new_plane):
        @pl.when(new_plane & (entry_class((t0 // 2) % 8) > mine))
        def _():
            pl.semaphore_wait(present.at[(t0 // 2) % 8], 8)

        for core in range(2):

            @pl.when(t0 + core != g)
            def _():
                send_copy(t0 + core).start()

    def transform(k, _):
        vis_copy(k).wait()
        chunk = chunk_of(k)
        turned[...] = lax.dot_general(
            table_v[...], vis_v[k], (((1,), (1,)), ((), ())), preferred_element_type=F32
        )
        for half in range(2):
            lanes = slice(half * LANES, (half + 1) * LANES)
            parts = [
                turned[pl.ds(pl.multiple_of(((h + NB - x) % 4) * ROWS, ROWS), ROWS), lanes]
                for h in range(4)
            ]
            rolled = []
            for d in range(4):
                v = pick(masks, [parts[(c + d) % 4] for c in range(4)])
                rolled.append(pltpu.roll(v, MB * d, 1) if d else v)
            for c in range(4):
                block = pick(masks, [rolled[(h - c) % 4] for h in range(4)])
                send[chunk * CHUNK + half * 4 + c] = block.astype(BF16)

        @pl.when(k == 0)
        def _():
            own_copy.start()
            flag_own.start()
            for o in range(1, NB):
                flag_copy(o).start()

        for dz in range(4):
            send_to(chunk * CHUNK + ((zl + dz) % 4) * 2, k % 4 == 0)

        @pl.when(k >= DELAY)
        def _():
            lax.fori_loop(4 * (k - DELAY), 4 * (k - DELAY + 1), step, 0)

        return 0

    def pair_of(k):
        dy, dz = (k // 4) % 4, k % 4
        return ((y + 4 - dy) % 4) * 16 + ((zh + k // 16) % 2) * 8 + ((zl + 4 - dz) % 4) * 2

    def x_copy(k, d):
        times = pl.ds(pair_of(k), 2)
        return pltpu.make_async_remote_copy(
            src_ref=gathered.at[0, times], dst_ref=gathered.at[(3, 1)[d], times],
            send_sem=x_s.at[d], recv_sem=x_r.at[d, k],
            device_id=(g, (right, left)[d]), device_id_type=MESH,
        )

    def f_copy(k, d):
        times = pl.ds(pair_of(k), 2)
        return pltpu.make_async_remote_copy(
            src_ref=gathered.at[(3, 1)[d], times], dst_ref=gathered.at[2, times],
            send_sem=f_s, recv_sem=f_r,
            device_id=(g, (right, left)[d]), device_id_type=MESH,
        )

    def step(k, _):
        @pl.when(k < NCELL)
        def _():
            for core in range(2):
                t = pair_of(k) + core

                @pl.when(t != g)
                def _():
                    arrival(t).wait_recv()

                @pl.when(t == g)
                def _():
                    own_copy.wait()

            x_copy(k, 0).start()
            x_copy(k, 1).start()

        @pl.when(k >= LAG)
        def _():
            m = k - LAG
            x_copy(m, 0).wait_recv()
            x_copy(m, 1).wait_recv()

            @pl.when(m % 2 == 0)
            def _():
                f_copy(m, 0).start()

            @pl.when(m % 2 == 1)
            def _():
                f_copy(m, 1).start()

        return 0

    lax.fori_loop(0, NCHUNK, transform, 0)
    lax.fori_loop(4 * (NCHUNK - DELAY), NCELL, step, 0)

    flag_own.wait()
    for o in range(1, NB):
        flag_copy(o).wait_recv()
    keep = keep_masks(flags)
    place_masks = group_masks((MB, LANES))

    def products(slots):
        for n, o in enumerate(slots):

            def widen(t, _):
                rows = pl.ds(pl.multiple_of(t * STRIDE, 8), ROWS)
                wide[rows, :] = gathered[o, t].astype(F32)
                return 0

            lax.fori_loop(0, NT, widen, 0, unroll=8)

            def relay(r, _):
                real = wide[pl.ds(2 * r, NT, stride=STRIDE), :]
                imag = wide[pl.ds(2 * r + 1, NT, stride=STRIDE), :]
                lanes = slice(n * LANES, (n + 1) * LANES)
                right_v[r, 0:NT, lanes] = real.astype(BF16)
                right_v[r, NT : 2 * NT, lanes] = imag.astype(BF16)
                if o == 0:
                    left_v[r, 0:LANES] = jnp.concatenate([real, imag], axis=0).T.astype(BF16)
                    left_v[r, LANES : 2 * LANES] = (
                        jnp.concatenate([imag, -real], axis=0).T.astype(BF16)
                    )
                return 0

            lax.fori_loop(0, NR, relay, 0, unroll=8)

        def multiply(r, _):
            x_all = jnp.dot(
                left_v[r], right_v[r, :, 0 : len(slots) * LANES], preferred_element_type=F32
            )
            for c in range(2):
                for ha in range(4):
                    rows = x_all[c * LANES + ha * MB : c * LANES + (ha + 1) * MB]
                    mask = place_masks[(ha + slots[0]) % 4]
                    value = rows[:, 0:LANES]
                    if len(slots) == 2:
                        value = jnp.where(mask, value, rows[:, LANES : 2 * LANES])
                        mask = mask | place_masks[(ha + slots[1]) % 4]
                    place = (r * 4 + (ha + NB - x) % 4) * MB
                    pltpu.store(
                        prod.at[c, pl.ds(pl.multiple_of(place, MB), MB), :],
                        value * keep[ha], mask=mask,
                    )
            return 0

        lax.fori_loop(0, NR, multiply, 0, unroll=8)

    products((0,))
    lax.fori_loop(NCELL, NCELL + LAG, step, 0)
    products((1, 3))

    def whole(slot, d, sent, received):
        return pltpu.make_async_remote_copy(
            src_ref=gathered.at[0], dst_ref=gathered.at[slot], send_sem=sent, recv_sem=received,
            device_id=(g, (right, left)[d]), device_id_type=MESH,
        )

    forwards = whole(2, 0, f_s, f_r)
    forwards.wait_recv()
    products((2,))
    forwards.wait_send()
    for d in range(2):
        whole((3, 1)[d], d, x_s.at[d], x_r.at[d, 0]).wait_send()
    pltpu.make_async_remote_copy(
        src_ref=send.at[pl.ds(0, NT - 1)], dst_ref=gathered.at[0, pl.ds(0, NT - 1)],
        send_sem=a_s, recv_sem=a_r.at[0], device_id=(g, right), device_id_type=MESH,
    ).wait_send()
    for o in range(1, NB):
        flag_copy(o).wait_send()


def keep_masks(flags):
    codes = []
    for o in range(NB):
        same = flags[o, 1:2, :] == flags[0, 1:2, :]
        codes.append(jnp.where(same, flags[o, 0:1, :], 0).astype(F32))
    own_valid = jnp.broadcast_to(flags[0, 0:1, :].astype(F32) / NT, (LANES, LANES)).T
    row_masks = group_masks((1, LANES))
    keep = []
    for ha in range(4):
        code = pick(row_masks, [codes[(hb - ha) % 4] for hb in range(4)])
        keep.append(own_valid[ha * MB : (ha + 1) * MB] * code)
    return keep


def turn_kernel(prod, out, out_v, out_sem):
    lane = lax.broadcasted_iota(jnp.int32, (MB, LANES), 1) % 4
    delay_masks = [lane == d for d in range(4)]

    def out_copy(n):
        c, i8 = n // 4, n % 4
        return pltpu.make_async_copy(
            out_v.at[:, c, pl.ds(i8 * 8, 8)], out.at[:, c, pl.ds(i8 * 8, 8)], out_sem.at[n]
        )

    for c in range(2):
        for i8 in range(4):

            def turn(ii, _):
                i = i8 * 8 + ii
                flat = prod[c, pl.ds(i, LANES, stride=MB), :].T
                for p in range(NB):
                    values = [flat[((d + p) % 4) * MB : ((d + p) % 4 + 1) * MB] for d in range(4)]
                    out_v[p, c, i] = pick(delay_masks, values)
                return 0

            lax.fori_loop(0, 8, turn, 0, unroll=8)
            out_copy(c * 4 + i8).start()
    for n in range(8):
        out_copy(n).wait()


def local(visibility, block_group, member_valid):
    vis = visibility.reshape(NT * MB, 2 * CH)
    table = jnp.asarray(delay_table())
    dma = pltpu.SemaphoreType.DMA
    hbm_spec = pl.BlockSpec(memory_space=pltpu.HBM)
    vmem_spec = pl.BlockSpec(memory_space=pltpu.VMEM)
    prod = pl.pallas_call(
        exchange_kernel,
        name="exchange",
        out_shape=jax.ShapeDtypeStruct((2, DBAND * MB, LANES), F32),
        in_specs=[hbm_spec] * 4,
        out_specs=vmem_spec,
        scratch_shapes=[
            pltpu.VMEM((NCHUNK, CHUNK * MB, 2 * CH), BF16),
            pltpu.VMEM((2 * DBAND, 2 * CH), BF16),
            pltpu.VMEM((1, MB), jnp.int32),
            pltpu.VMEM((1, 1), jnp.int32),
            pltpu.VMEM((2 * DBAND, CHUNK * MB), F32),
            pltpu.VMEM((NT, ROWS, LANES), BF16),
            pltpu.VMEM((8, LANES), jnp.int32),
            pltpu.VMEM((NB, 8, LANES), jnp.int32),
            pltpu.VMEM((NB, NT, ROWS, LANES), BF16),
            pltpu.VMEM((NT * STRIDE, LANES), F32),
            pltpu.VMEM((NR, 2 * NT, 2 * LANES), BF16),
            pltpu.VMEM((NR, 2 * LANES, 2 * NT), BF16),
            dma((NCHUNK,)), dma, dma, dma, dma, dma,
            pltpu.SemaphoreType.REGULAR((NZ,)),
            dma, dma((NT,)),
            dma((2,)), dma((2, NCELL)),
            dma, dma,
            dma((NB,)), dma((NB,)),
        ],
        compiler_params=pltpu.CompilerParams(
            collective_id=0, has_side_effects=True, vmem_limit_bytes=EXCHANGE_VMEM
        ),
    )(
        *(
            pltpu.with_memory_space_constraint(a, pltpu.HBM)
            for a in (vis, table, member_valid.reshape(1, MB))
        ),
        block_group.reshape(1, 1),
    )
    result = pl.pallas_call(
        turn_kernel,
        name="turn",
        out_shape=jax.ShapeDtypeStruct((NB, 2, MB, MB, DBAND), F32),
        in_specs=[vmem_spec],
        out_specs=hbm_spec,
        scratch_shapes=[pltpu.VMEM((NB, 2, MB, MB, DBAND), F32), dma((8,))],
        compiler_params=pltpu.CompilerParams(vmem_limit_bytes=TURN_VMEM),
    )(prod)
    return result[None, None]


def solution(mesh):
    in_specs = (P("grp", "blk", None, None, None), P("blk", "grp"), P("blk", "grp", None))
    out_specs = P("blk", "grp", None, None, None, None, None)
    return jax.shard_map(local, mesh=mesh, in_specs=in_specs, out_specs=out_specs, check_vma=False)
```

```python
import functools
import math

import jax
import jax.numpy as jnp
import numpy as np
import ml_dtypes
from jax import lax
from jax.experimental import pallas as pl
from jax.experimental.pallas import tpu as pltpu
from jax.sharding import PartitionSpec as P

MESH = pl.DeviceIdType.MESH
F32 = jnp.float32
BF16 = jnp.bfloat16

CH = 1024
DBAND = 128
MB = 32
NT = 64
NB = 4
NY, NZ = 4, 8
ROWS = 64
LANES = 128
NR = DBAND // 4
CHUNK = 8
NCHUNK = NT // CHUNK
NCELL = NT // 2
LAG = 8
DELAY = 3
EXCHANGE_VMEM = 48 << 20
TURN_VMEM = 16 << 20
STRIDE = 68


def delay_table():
    f = np.arange(CH)
    angles = 2.0 * math.pi * f / CH
    window = (
        0.35875
        - 0.48829 * np.cos(angles)
        + 0.14128 * np.cos(2.0 * angles)
        - 0.01168 * np.cos(3.0 * angles)
    ).astype(np.float32)
    d = np.arange(DBAND) - DBAND // 2
    phases = 2.0 * math.pi * ((f[:, None] * d[None, :]) % CH) / CH
    scaling = window[:, None].astype(np.float64) / math.sqrt(CH)
    c, s = scaling * np.cos(phases), scaling * np.sin(phases)
    real = np.concatenate([c, s], axis=0)
    imag = np.concatenate([-s, c], axis=0)
    both = np.stack([real, imag], axis=2).reshape(2 * CH, NR, 4, 2)
    rows = both.transpose(2, 1, 3, 0).reshape(2 * DBAND, 2 * CH)
    return rows.astype(np.float32).astype(ml_dtypes.bfloat16)


def entry_class(z):
    return z - (z // 4) * (z - 4)


def group_masks(shape):
    group = lax.broadcasted_iota(jnp.int32, shape, 1) // MB
    return [group == h for h in range(4)]


def pick(masks, values):
    out = values[3]
    for h in (2, 1, 0):
        out = jnp.where(masks[h], values[h], out)
    return out


def exchange_kernel(
    vis, table, valid, label, prod,
    vis_v, table_v, valid_v, label_v, turned, send, own_flags, flags, gathered, wide, right_v, left_v,
    vis_sem, table_sem, valid_sem, label_sem, own_sem, flag_own_sem,
    present, a_s, a_r, x_s, x_r, f_s, f_r, g_s, g_r,
):
    g = lax.axis_index("grp")
    x = lax.axis_index("blk")
    y, z, zh, zl = g // 16, (g // 2) % 8, (g // 8) % 2, (g // 2) % 4
    right, left = (x + 1) % 4, (x + 3) % 4

    def chunk_of(k):
        return ((y + k) % 4) * 2 + (zh + k // 4) % 2

    def vis_copy(k):
        rows = pl.ds(pl.multiple_of(chunk_of(k) * CHUNK * MB, CHUNK * MB), CHUNK * MB)
        return pltpu.make_async_copy(vis.at[rows], vis_v.at[k], vis_sem.at[k])

    table_copy = pltpu.make_async_copy(table, table_v, table_sem)
    valid_copy = pltpu.make_async_copy(valid, valid_v, valid_sem)
    label_copy = pltpu.make_async_copy(label, label_v, label_sem)
    table_copy.start()
    valid_copy.start()
    label_copy.start()
    for k in range(NCHUNK):
        vis_copy(k).start()

    barrier = pltpu.get_barrier_semaphore()

    mine = entry_class(z)

    def plane(pz, sem):
        for py in range(NY):
            for core in range(2):
                t = py * 16 + pz * 2 + core

                @pl.when(t != g)
                def _():
                    pl.semaphore_signal(sem, inc=1, device_id=(t, x), device_id_type=MESH)

    lax.fori_loop(mine, NZ, lambda pz, _: (plane(pz, barrier), 0)[1], 0)
    for o in range(1, NB):
        pl.semaphore_signal(barrier, inc=1, device_id=(g, (x + o) % NB), device_id_type=MESH)
    last = mine + 1 + (z // 4) * 3
    pl.semaphore_wait(barrier, last * 8 - 1 + NB - 1)
    lax.fori_loop(0, mine, lambda pz, _: (plane(pz, present.at[z]), 0)[1], 0)

    valid_copy.wait()
    label_copy.wait()
    own_flags[...] = jnp.zeros_like(own_flags)
    own_flags[0:1, :] = jnp.concatenate([valid_v[...]] * 4, axis=1)
    own_flags[1:2, :] = jnp.broadcast_to(label_v[...], (1, LANES))
    table_copy.wait()

    def send_copy(t):
        return pltpu.make_async_remote_copy(
            src_ref=send.at[t], dst_ref=gathered.at[0, g],
            send_sem=a_s, recv_sem=a_r.at[g],
            device_id=(t, x), device_id_type=MESH,
        )

    def arrival(t):
        return pltpu.make_async_remote_copy(
            src_ref=send.at[t], dst_ref=gathered.at[0, t],
            send_sem=a_s, recv_sem=a_r.at[t],
            device_id=(t, x), device_id_type=MESH,
        )

    own_copy = pltpu.make_async_copy(send.at[g], gathered.at[0, g], own_sem)
    flag_own = pltpu.make_async_copy(own_flags, flags.at[0], flag_own_sem)
    masks = group_masks((ROWS, LANES))

    def flag_copy(o):
        return pltpu.make_async_remote_copy(
            src_ref=own_flags, dst_ref=flags.at[o],
            send_sem=g_s.at[o], recv_sem=g_r.at[o],
            device_id=(g, (x + NB - o) % NB), device_id_type=MESH,
        )

    def send_to(t0, new_plane):
        @pl.when(new_plane & (entry_class((t0 // 2) % 8) > mine))
        def _():
            pl.semaphore_wait(present.at[(t0 // 2) % 8], 8)

        for core in range(2):

            @pl.when(t0 + core != g)
            def _():
                send_copy(t0 + core).start()

    def transform(k, _):
        vis_copy(k).wait()
        chunk = chunk_of(k)
        turned[...] = lax.dot_general(
            table_v[...], vis_v[k], (((1,), (1,)), ((), ())), preferred_element_type=F32
        )
        for half in range(2):
            lanes = slice(half * LANES, (half + 1) * LANES)
            parts = [
                turned[pl.ds(pl.multiple_of(((h + NB - x) % 4) * ROWS, ROWS), ROWS), lanes]
                for h in range(4)
            ]
            rolled = []
            for d in range(4):
                v = pick(masks, [parts[(c + d) % 4] for c in range(4)])
                rolled.append(pltpu.roll(v, MB * d, 1) if d else v)
            for c in range(4):
                block = pick(masks, [rolled[(h - c) % 4] for h in range(4)])
                send[chunk * CHUNK + half * 4 + c] = block.astype(BF16)

        @pl.when(k == 0)
        def _():
            own_copy.start()
            flag_own.start()
            for o in range(1, NB):
                flag_copy(o).start()

        for dz in range(4):
            send_to(chunk * CHUNK + ((zl + dz) % 4) * 2, k % 4 == 0)

        @pl.when(k >= DELAY)
        def _():
            lax.fori_loop(4 * (k - DELAY), 4 * (k - DELAY + 1), step, 0)

        return 0

    def pair_of(k):
        dy, dz = (k // 4) % 4, k % 4
        return ((y + 4 - dy) % 4) * 16 + ((zh + k // 16) % 2) * 8 + ((zl + 4 - dz) % 4) * 2

    def x_copy(k, d):
        times = pl.ds(pair_of(k), 2)
        return pltpu.make_async_remote_copy(
            src_ref=gathered.at[0, times], dst_ref=gathered.at[(3, 1)[d], times],
            send_sem=x_s.at[d], recv_sem=x_r.at[d, k],
            device_id=(g, (right, left)[d]), device_id_type=MESH,
        )

    def f_copy(k, d):
        times = pl.ds(pair_of(k), 2)
        return pltpu.make_async_remote_copy(
            src_ref=gathered.at[(3, 1)[d], times], dst_ref=gathered.at[2, times],
            send_sem=f_s, recv_sem=f_r,
            device_id=(g, (right, left)[d]), device_id_type=MESH,
        )

    def step(k, _):
        @pl.when(k < NCELL)
        def _():
            for core in range(2):
                t = pair_of(k) + core

                @pl.when(t != g)
                def _():
                    arrival(t).wait_recv()

                @pl.when(t == g)
                def _():
                    own_copy.wait()

            x_copy(k, 0).start()
            x_copy(k, 1).start()

        @pl.when(k >= LAG)
        def _():
            m = k - LAG
            x_copy(m, 0).wait_recv()
            x_copy(m, 1).wait_recv()

            @pl.when(m % 2 == 0)
            def _():
                f_copy(m, 0).start()

            @pl.when(m % 2 == 1)
            def _():
                f_copy(m, 1).start()

        return 0

    lax.fori_loop(0, NCHUNK, transform, 0)
    lax.fori_loop(4 * (NCHUNK - DELAY), NCELL, step, 0)

    flag_own.wait()
    for o in range(1, NB):
        flag_copy(o).wait_recv()
    keep = keep_masks(flags)
    place_masks = group_masks((MB, LANES))

    def products(slots):
        for n, o in enumerate(slots):

            for t in range(NT):
                wide[t * STRIDE : t * STRIDE + ROWS, :] = gathered[o, t].astype(F32)

            def relay(r, _):
                real = wide[pl.ds(2 * r, NT, stride=STRIDE), :]
                imag = wide[pl.ds(2 * r + 1, NT, stride=STRIDE), :]
                lanes = slice(n * LANES, (n + 1) * LANES)
                right_v[r, 0:NT, lanes] = real.astype(BF16)
                right_v[r, NT : 2 * NT, lanes] = imag.astype(BF16)
                if o == 0:
                    left_v[r, 0:LANES] = jnp.concatenate([real, imag], axis=0).T.astype(BF16)
                    left_v[r, LANES : 2 * LANES] = (
                        jnp.concatenate([imag, -real], axis=0).T.astype(BF16)
                    )
                return 0

            lax.fori_loop(0, NR, relay, 0, unroll=8)

        def multiply(r, _):
            x_all = jnp.dot(
                left_v[r], right_v[r, :, 0 : len(slots) * LANES], preferred_element_type=F32
            )
            for c in range(2):
                for ha in range(4):
                    rows = x_all[c * LANES + ha * MB : c * LANES + (ha + 1) * MB]
                    mask = place_masks[(ha + slots[0]) % 4]
                    value = rows[:, 0:LANES]
                    if len(slots) == 2:
                        value = jnp.where(mask, value, rows[:, LANES : 2 * LANES])
                        mask = mask | place_masks[(ha + slots[1]) % 4]
                    place = (r * 4 + (ha + NB - x) % 4) * MB
                    pltpu.store(
                        prod.at[c, pl.ds(pl.multiple_of(place, MB), MB), :],
                        value * keep[ha], mask=mask,
                    )
            return 0

        lax.fori_loop(0, NR, multiply, 0, unroll=8)

    products((0,))
    lax.fori_loop(NCELL, NCELL + LAG, step, 0)
    products((1, 3))

    def whole(slot, d, sent, received):
        return pltpu.make_async_remote_copy(
            src_ref=gathered.at[0], dst_ref=gathered.at[slot], send_sem=sent, recv_sem=received,
            device_id=(g, (right, left)[d]), device_id_type=MESH,
        )

    forwards = whole(2, 0, f_s, f_r)
    forwards.wait_recv()
    products((2,))
    forwards.wait_send()
    for d in range(2):
        whole((3, 1)[d], d, x_s.at[d], x_r.at[d, 0]).wait_send()
    pltpu.make_async_remote_copy(
        src_ref=send.at[pl.ds(0, NT - 1)], dst_ref=gathered.at[0, pl.ds(0, NT - 1)],
        send_sem=a_s, recv_sem=a_r.at[0], device_id=(g, right), device_id_type=MESH,
    ).wait_send()
    for o in range(1, NB):
        flag_copy(o).wait_send()


def keep_masks(flags):
    codes = []
    for o in range(NB):
        same = flags[o, 1:2, :] == flags[0, 1:2, :]
        codes.append(jnp.where(same, flags[o, 0:1, :], 0).astype(F32))
    own_valid = jnp.broadcast_to(flags[0, 0:1, :].astype(F32) / NT, (LANES, LANES)).T
    row_masks = group_masks((1, LANES))
    keep = []
    for ha in range(4):
        code = pick(row_masks, [codes[(hb - ha) % 4] for hb in range(4)])
        keep.append(own_valid[ha * MB : (ha + 1) * MB] * code)
    return keep


def turn_kernel(prod, out, out_v, out_sem):
    lane = lax.broadcasted_iota(jnp.int32, (MB, LANES), 1) % 4
    delay_masks = [lane == d for d in range(4)]

    def out_copy(n):
        c, i8 = n // 4, n % 4
        return pltpu.make_async_copy(
            out_v.at[:, c, pl.ds(i8 * 8, 8)], out.at[:, c, pl.ds(i8 * 8, 8)], out_sem.at[n]
        )

    for c in range(2):
        for i8 in range(4):

            def turn(ii, _):
                i = i8 * 8 + ii
                flat = prod[c, pl.ds(i, LANES, stride=MB), :].T
                for p in range(NB):
                    values = [flat[((d + p) % 4) * MB : ((d + p) % 4 + 1) * MB] for d in range(4)]
                    out_v[p, c, i] = pick(delay_masks, values)
                return 0

            lax.fori_loop(0, 8, turn, 0, unroll=8)
            out_copy(c * 4 + i8).start()
    for n in range(8):
        out_copy(n).wait()


def local(visibility, block_group, member_valid):
    vis = visibility.reshape(NT * MB, 2 * CH)
    table = jnp.asarray(delay_table())
    dma = pltpu.SemaphoreType.DMA
    hbm_spec = pl.BlockSpec(memory_space=pltpu.HBM)
    vmem_spec = pl.BlockSpec(memory_space=pltpu.VMEM)
    prod = pl.pallas_call(
        exchange_kernel,
        name="exchange",
        out_shape=jax.ShapeDtypeStruct((2, DBAND * MB, LANES), F32),
        in_specs=[hbm_spec] * 4,
        out_specs=vmem_spec,
        scratch_shapes=[
            pltpu.VMEM((NCHUNK, CHUNK * MB, 2 * CH), BF16),
            pltpu.VMEM((2 * DBAND, 2 * CH), BF16),
            pltpu.VMEM((1, MB), jnp.int32),
            pltpu.VMEM((1, 1), jnp.int32),
            pltpu.VMEM((2 * DBAND, CHUNK * MB), F32),
            pltpu.VMEM((NT, ROWS, LANES), BF16),
            pltpu.VMEM((8, LANES), jnp.int32),
            pltpu.VMEM((NB, 8, LANES), jnp.int32),
            pltpu.VMEM((NB, NT, ROWS, LANES), BF16),
            pltpu.VMEM((NT * STRIDE, LANES), F32),
            pltpu.VMEM((NR, 2 * NT, 2 * LANES), BF16),
            pltpu.VMEM((NR, 2 * LANES, 2 * NT), BF16),
            dma((NCHUNK,)), dma, dma, dma, dma, dma,
            pltpu.SemaphoreType.REGULAR((NZ,)),
            dma, dma((NT,)),
            dma((2,)), dma((2, NCELL)),
            dma, dma,
            dma((NB,)), dma((NB,)),
        ],
        compiler_params=pltpu.CompilerParams(
            collective_id=0, has_side_effects=True, vmem_limit_bytes=EXCHANGE_VMEM
        ),
    )(
        *(
            pltpu.with_memory_space_constraint(a, pltpu.HBM)
            for a in (vis, table, member_valid.reshape(1, MB))
        ),
        block_group.reshape(1, 1),
    )
    result = pl.pallas_call(
        turn_kernel,
        name="turn",
        out_shape=jax.ShapeDtypeStruct((NB, 2, MB, MB, DBAND), F32),
        in_specs=[vmem_spec],
        out_specs=hbm_spec,
        scratch_shapes=[pltpu.VMEM((NB, 2, MB, MB, DBAND), F32), dma((8,))],
        compiler_params=pltpu.CompilerParams(vmem_limit_bytes=TURN_VMEM),
    )(prod)
    return result[None, None]


def solution(mesh):
    in_specs = (P("grp", "blk", None, None, None), P("blk", "grp"), P("blk", "grp", None))
    out_specs = P("blk", "grp", None, None, None, None, None)
    return jax.shard_map(local, mesh=mesh, in_specs=in_specs, out_specs=out_specs, check_vma=False)
```
